32 devices in a mesh: blk: 4 (over x, core), sub: 8 (over z, y).
Axes of the slice: x: 2, y: 2, z: 4, core: 2. Of those that a mesh axis runs over, the one named last changes fastest.
Arguments:
- images: bfloat16 [16384, 768], P(('blk', 'sub')), may hold values from -6 to 6
- texts: bfloat16 [16384, 768], P(('blk', 'sub')), may hold values from -6 to 6
- logit_scale: float32 [1], replicated, may hold values from 2 to 10
- logit_bias: float32 [1], replicated, may hold values from -4 to -1
Outputs:
- grad_images: float32 [16384, 768], P(('blk', 'sub'))
- grad_texts: float32 [16384, 768], P(('blk', 'sub'))
The draws below stay inside these ranges and needn't reach their ends.
All inputs are finite; a program needn't handle non-finite values.
Results may differ from the reference program's by a relative error of at most 0.004.
Values may be sent and summed in bfloat16 or wider, within the bound.
No kernel may reach another device: no remote copies, remote signals or barrier semaphores. Data moves between devices by JAX's collectives and lax.ppermute only.
A program may use at most 64 MiB of HBM per device.

```python
import math
import jax
import jax.numpy as jnp
from jax import lax

EMBED = 768
B_DEV = 512
N_ROWS = 16384
N_BLK = 4
N_SUB = 8


def block_levels(rng, extent, pieces, least, high):
    loudness, own = 1.0, jax.random.fold_in(rng, 6)
    for axis_at, shards_of in pieces:
        heights = jnp.exp(jax.random.uniform(jax.random.fold_in(own, axis_at), (shards_of,), jnp.float32, least / len(pieces), high / len(pieces)))
        loudness = loudness * jnp.repeat(heights, extent[axis_at] // shards_of).reshape([-1 if axis == axis_at else 1 for axis in range(len(extent))])
    return loudness


def scatter_about(stream_key, shape, scale, reach, split=(), held_as=jnp.bfloat16):
    values = jax.random.normal(stream_key, shape, jnp.float32) * scale
    if len(split) > 0:
        values = block_levels(stream_key, shape, split, -0.22, 0.18) * values
    return jnp.clip(values, min=-reach, max=reach).astype(held_as)


def setup_inputs(seed: int = 0) -> dict:
    key_list = jax.random.split(jax.random.key(seed), 5)
    return {
        "images": scatter_about(key_list[0], (N_ROWS, EMBED), 1.0, 6.0, ((0, 32),)),
        "texts": scatter_about(key_list[1], (N_ROWS, EMBED), 1.0, 6.0, ((0, 32),)),
        "logit_scale": jnp.clip(jnp.exp(jax.random.uniform(key_list[2], (1,), jnp.float32, math.log(2.0), math.log(10.0))), 2.0, 10.0),
        "logit_bias": jnp.clip(jax.random.uniform(key_list[3], (1,), jnp.float32, -4.0, -1.0), -4.0, -1.0),
    }


def unit_rows(values_in):
    values = values_in.astype(jnp.float32)
    recip = lax.rsqrt(lax.optimization_barrier(jnp.sum(values * values, axis=-1, keepdims=True)) + 1e-06)
    return (values * recip, recip)

def tile_weights(left, right, scale, offset):
    logits = scale * jnp.dot(left, right.T, preferred_element_type=jnp.float32) + offset
    return jax.nn.sigmoid(logits)

def contract_rows(weights, rows):
    return lax.dot_general(weights, rows, (((0,), (0,)), ((), ())), preferred_element_type=jnp.float32)

def back_norm(unit, recip, grad):
    return (grad - unit * lax.optimization_barrier(jnp.sum(unit * grad, axis=-1, keepdims=True))) * recip

def reference(images, texts, logit_scale, logit_bias):
    count = N_BLK * N_SUB
    unit_img, recip_img = unit_rows(images)
    unit_txt, recip_txt = unit_rows(texts)
    img_low = unit_img.astype(jnp.bfloat16).reshape(count, B_DEV, EMBED)
    txt_low = unit_txt.astype(jnp.bfloat16).reshape(count, B_DEV, EMBED)
    scale = logit_scale[0]
    offset = logit_bias[0]
    diagonal_one = jnp.eye(B_DEV, dtype=jnp.float32)

    def per_block(block_set):
        img_own, img_prev, img_next, txt_own, txt_prev, txt_next = block_set
        weight_own = (tile_weights(img_own, txt_own, scale, offset) - diagonal_one).astype(jnp.bfloat16)
        weight_prev = tile_weights(img_own, txt_prev, scale, offset).astype(jnp.bfloat16)
        weight_next = tile_weights(img_own, txt_next, scale, offset).astype(jnp.bfloat16)
        from_prev = tile_weights(img_prev, txt_own, scale, offset).astype(jnp.bfloat16)
        from_next = tile_weights(img_next, txt_own, scale, offset).astype(jnp.bfloat16)
        grad_img = scale * (jnp.dot(weight_own, txt_own, preferred_element_type=jnp.float32) + jnp.dot(weight_prev, txt_prev, preferred_element_type=jnp.float32) + jnp.dot(weight_next, txt_next, preferred_element_type=jnp.float32))
        grad_txt = scale * (contract_rows(weight_own, img_own) + contract_rows(from_prev, img_prev) + contract_rows(from_next, img_next))
        return (grad_img, grad_txt)
    grad_img, grad_txt = lax.map(per_block, (img_low, jnp.roll(img_low, 1, 0), jnp.roll(img_low, -1, 0), txt_low, jnp.roll(txt_low, 1, 0), jnp.roll(txt_low, -1, 0)))
    grad_img = grad_img.reshape(-1, EMBED)
    grad_txt = grad_txt.reshape(-1, EMBED)
    return (back_norm(unit_img, recip_img, grad_img), back_norm(unit_txt, recip_txt, grad_txt))
```

```python
import functools

import jax
import jax.numpy as jnp
from jax import lax
from jax.experimental import pallas as pl
from jax.experimental.pallas import tpu as pltpu
from jax.sharding import PartitionSpec as P

AXES = ("blk", "sub")
LAST = (((1,), (1,)), ((), ()))
FIRST = (((0,), (0,)), ((), ()))
VMEM_LIMIT = 24 * 1024 * 1024


def unit_rows(values_in):
    values = values_in.astype(jnp.float32)
    recip = lax.rsqrt(jnp.sum(values * values, axis=-1, keepdims=True) + 1e-06)
    return values * recip, recip


def dot32(left, right, dims):
    return lax.dot_general(left, right, dims, preferred_element_type=jnp.float32)


def band_term(own_low, other_low, scale, offset):
    weight = jax.nn.sigmoid(scale * dot32(own_low, other_low, LAST) + offset)
    return jnp.dot(
        weight.astype(jnp.bfloat16), other_low, preferred_element_type=jnp.float32
    )


def own_kernel(scale_ref, offset_ref, img_ref, txt_ref, img_low, txt_low, sum_img, sum_txt):
    scale, offset = scale_ref[0], offset_ref[0]
    img_low[...] = unit_rows(img_ref[...])[0].astype(jnp.bfloat16)
    txt_low[...] = unit_rows(txt_ref[...])[0].astype(jnp.bfloat16)
    logits = scale * dot32(img_low[...], txt_low[...], LAST) + offset
    rows = lax.broadcasted_iota(jnp.int32, logits.shape, 0)
    columns = lax.broadcasted_iota(jnp.int32, logits.shape, 1)
    weight = jax.nn.sigmoid(logits) - (rows == columns).astype(jnp.float32)
    weight = weight.astype(jnp.bfloat16)
    sum_img[...] = jnp.dot(weight, txt_low[...], preferred_element_type=jnp.float32)
    sum_txt[...] = dot32(weight, img_low[...], FIRST)


def add_kernel(scale_ref, offset_ref, low_ref, other_ref, sum_in, sum_out, other_low):
    scale, offset = scale_ref[0], offset_ref[0]
    other_low[...] = unit_rows(other_ref[...])[0].astype(jnp.bfloat16)
    sum_out[...] = sum_in[...] + band_term(low_ref[...], other_low[...], scale, offset)


def last_kernel(count, scale_ref, offset_ref, raw_ref, low_ref, sum_ref, *rest):
    others, (out_ref, other_low) = rest[:count], rest[count:]
    scale, offset = scale_ref[0], offset_ref[0]

    @pl.when(pl.program_id(0) == 0)
    def _():
        at = 0
        for other in others:
            rows = other.shape[0]
            other_low[at : at + rows, :] = unit_rows(other[...])[0].astype(jnp.bfloat16)
            at += rows

    total = sum_ref[...] + band_term(low_ref[...], other_low[...], scale, offset)
    grad = scale * total
    unit, recip = unit_rows(raw_ref[...])
    out_ref[...] = (grad - unit * jnp.sum(unit * grad, axis=-1, keepdims=True)) * recip


def cost(own, others, width, flops_scale=1.0):
    return pl.CostEstimate(
        flops=int(4 * own * others * width * flops_scale),
        bytes_accessed=own * width * 10 + others * width * 2,
        transcendentals=own * others,
    )


SMEM = pl.BlockSpec(memory_space=pltpu.SMEM)
VMEM = pl.BlockSpec(memory_space=pltpu.VMEM)
PARAMS = pltpu.CompilerParams(vmem_limit_bytes=VMEM_LIMIT)


def own_call(scale, offset, images, texts):
    rows, width = images.shape
    low = jax.ShapeDtypeStruct((rows, width), jnp.bfloat16)
    total = jax.ShapeDtypeStruct((rows, width), jnp.float32)
    return pl.pallas_call(
        own_kernel,
        out_shape=(low, low, total, total),
        in_specs=[SMEM, SMEM, VMEM, VMEM],
        out_specs=(VMEM,) * 4,
        compiler_params=PARAMS,
        cost_estimate=cost(rows, rows, width, 1.5),
    )(scale, offset, images, texts)


def add_call(scale, offset, low, other, total):
    rows, width = low.shape
    return pl.pallas_call(
        add_kernel,
        out_shape=jax.ShapeDtypeStruct((rows, width), jnp.float32),
        in_specs=[SMEM, SMEM, VMEM, VMEM, VMEM],
        out_specs=VMEM,
        scratch_shapes=[pltpu.VMEM(other.shape, jnp.bfloat16)],
        input_output_aliases={4: 0},
        compiler_params=PARAMS,
        cost_estimate=cost(rows, other.shape[0], width),
    )(scale, offset, low, other, total)


def last_call(scale, offset, raw, low, total, others):
    rows, width = raw.shape
    steps = 4 if rows % 64 == 0 else 1
    block = pl.BlockSpec((rows // steps, width), lambda step: (step, 0))
    count = sum(other.shape[0] for other in others)
    return pl.pallas_call(
        functools.partial(last_kernel, len(others)),
        grid=(steps,),
        out_shape=jax.ShapeDtypeStruct((rows, width), jnp.float32),
        in_specs=[SMEM, SMEM, block, block, block] + [VMEM] * len(others),
        out_specs=block,
        scratch_shapes=[pltpu.VMEM((count, width), jnp.bfloat16)],
        compiler_params=PARAMS,
        cost_estimate=cost(rows, count, width),
    )(scale, offset, raw, low, total, *others)


def exchange(value, target):
    count = lax.axis_size(AXES)
    return lax.ppermute(value, AXES, [(at, target(at) % count) for at in range(count)])


def partner(at):
    return at ^ 1


def onward(at):
    return at + 2 if at % 2 == 0 else at - 2


def backward(at):
    return at - 2 if at % 2 == 0 else at + 2


def tied(value, *others):
    return lax.optimization_barrier((value, *others))[0]


def shards(images, texts, logit_scale, logit_bias):
    rows = images.shape[0]
    cut = rows * 3 // 4
    rest = rows - cut
    args = (logit_scale, logit_bias)
    txt_head, img_head = texts[:cut], images[:cut]
    tails = jnp.concatenate([texts[cut:], images[cut:]], axis=0)

    near_txt = exchange(txt_head, partner)
    near_img = exchange(img_head, partner)
    side = exchange(tails, backward)

    img_low, txt_low, sum_img, sum_txt = own_call(*args, images, texts)

    far_txt = exchange(near_txt, onward)
    near_tails = exchange(tied(tails, near_txt), partner)
    far_tails = exchange(tied(side, near_txt), partner)
    sum_img = add_call(*args, img_low, near_txt, sum_img)

    far_img = exchange(near_img, onward)
    sum_txt = add_call(*args, txt_low, near_img, sum_txt)
    sum_img = add_call(*args, img_low, far_txt, sum_img)

    grad_img = last_call(
        *args, images, img_low, sum_img, (near_tails[:rest], far_tails[:rest])
    )
    grad_txt = last_call(
        *args, texts, txt_low, sum_txt, (near_tails[rest:], far_tails[rest:], far_img)
    )
    return grad_img, grad_txt


def solution(mesh):
    split = P(AXES, None)
    return jax.shard_map(
        shards,
        mesh=mesh,
        in_specs=(split, split, P(), P()),
        out_specs=(split, split),
        check_vma=False,
    )
```

```python
import functools

import jax
import jax.numpy as jnp
from jax import lax
from jax.experimental import pallas as pl
from jax.experimental.pallas import tpu as pltpu
from jax.sharding import PartitionSpec as P

AXES = ("blk", "sub")
LAST = (((1,), (1,)), ((), ()))
FIRST = (((0,), (0,)), ((), ()))
VMEM_LIMIT = 24 * 1024 * 1024


def unit_rows(values_in):
    values = values_in.astype(jnp.float32)
    recip = lax.rsqrt(jnp.sum(values * values, axis=-1, keepdims=True) + 1e-06)
    return values * recip, recip


def dot32(left, right, dims):
    return lax.dot_general(left, right, dims, preferred_element_type=jnp.float32)


def band_term(own_low, other_low, scale, offset):
    weight = jax.nn.sigmoid(scale * dot32(own_low, other_low, LAST) + offset)
    return jnp.dot(
        weight.astype(jnp.bfloat16), other_low, preferred_element_type=jnp.float32
    )


def take_kernel(value_ref, out_ref, sem):
    copy = pltpu.make_async_copy(value_ref.at[pl.ds(0, out_ref.shape[0]), :], out_ref, sem)
    copy.start()
    copy.wait()


def own_kernel(scale_ref, offset_ref, img_ref, txt_ref, img_low, txt_low, sum_img, sum_txt):
    scale, offset = scale_ref[0], offset_ref[0]
    lower_rows((img_ref,), img_low)
    lower_rows((txt_ref,), txt_low)
    logits = scale * dot32(img_low[...], txt_low[...], LAST) + offset
    rows = lax.broadcasted_iota(jnp.int32, logits.shape, 0)
    columns = lax.broadcasted_iota(jnp.int32, logits.shape, 1)
    weight = jax.nn.sigmoid(logits) - (rows == columns).astype(jnp.float32)
    weight = weight.astype(jnp.bfloat16)
    sum_img[...] = jnp.dot(weight, txt_low[...], preferred_element_type=jnp.float32)
    sum_txt[...] = dot32(weight, img_low[...], FIRST)


def lower_rows(others, other_low):
    at = 0
    for other in others:
        rows = other.shape[0]
        other_low[at : at + rows, :] = unit_rows(other[...])[0].astype(jnp.bfloat16)
        at += rows


def add_kernel(count, scale_ref, offset_ref, low_ref, sum_in, *rest):
    others, (sum_out, other_low) = rest[:count], rest[count:]
    scale, offset = scale_ref[0], offset_ref[0]
    lower_rows(others, other_low)
    sum_out[...] = sum_in[...] + band_term(low_ref[...], other_low[...], scale, offset)


def last_kernel(count, blocks, scale_ref, offset_ref, raw_ref, low_ref, sum_ref, *rest):
    others, (out_ref, other_low, held, sems) = rest[:count], rest[count:]
    scale, offset = scale_ref[0], offset_ref[0]
    lower_rows(others, other_low)
    size = held.shape[0] // blocks
    copies = []
    for block in range(blocks):
        at = pl.ds(block * size, size)
        unit, recip = unit_rows(raw_ref[at, :])
        total = sum_ref[at, :] + band_term(low_ref[at, :], other_low[...], scale, offset)
        grad = scale * total
        along = jnp.sum(unit * grad, axis=-1, keepdims=True)
        held[at, :] = (grad - unit * along) * recip
        copy = pltpu.make_async_copy(held.at[at, :], out_ref.at[at, :], sems.at[block])
        copy.start()
        copies.append(copy)
    for copy in copies:
        copy.wait()


def cost(micros):
    return pl.CostEstimate(flops=int(micros * 1e9), bytes_accessed=1024, transcendentals=0)


SMEM = pl.BlockSpec(memory_space=pltpu.SMEM)
VMEM = pl.BlockSpec(memory_space=pltpu.VMEM)
PARAMS = pltpu.CompilerParams(vmem_limit_bytes=VMEM_LIMIT)


def take_call(value, count):
    return pl.pallas_call(
        take_kernel,
        out_shape=jax.ShapeDtypeStruct((count, value.shape[1]), value.dtype),
        in_specs=[pl.BlockSpec(memory_space=pl.ANY)],
        out_specs=VMEM,
        scratch_shapes=[pltpu.SemaphoreType.DMA],
        compiler_params=PARAMS,
        cost_estimate=cost(0.05),
    )(value)


def own_call(scale, offset, images, texts):
    rows, width = texts.shape
    low = jax.ShapeDtypeStruct((rows, width), jnp.bfloat16)
    total = jax.ShapeDtypeStruct((rows, width), jnp.float32)
    return pl.pallas_call(
        own_kernel,
        out_shape=(low, low, total, total),
        in_specs=[SMEM, SMEM, VMEM, VMEM],
        out_specs=(VMEM,) * 4,
        compiler_params=PARAMS,
        cost_estimate=cost(0.05),
    )(scale, offset, images, texts)


def add_call(scale, offset, low, total, others, micros):
    rows, width = low.shape
    count = sum(other.shape[0] for other in others)
    return pl.pallas_call(
        functools.partial(add_kernel, len(others)),
        out_shape=jax.ShapeDtypeStruct((rows, width), jnp.float32),
        in_specs=[SMEM, SMEM] + [VMEM] * (2 + len(others)),
        out_specs=VMEM,
        scratch_shapes=[pltpu.VMEM((count, width), jnp.bfloat16)],
        input_output_aliases={3: 0},
        compiler_params=PARAMS,
        cost_estimate=cost(micros),
    )(scale, offset, low, total, *others)


def last_call(scale, offset, raw, low, total, others, micros):
    rows, width = raw.shape
    count = sum(other.shape[0] for other in others)
    blocks = 2 if rows % 32 == 0 else 1
    return pl.pallas_call(
        functools.partial(last_kernel, len(others), blocks),
        out_shape=jax.ShapeDtypeStruct((rows, width), jnp.float32),
        in_specs=[SMEM, SMEM] + [VMEM] * (3 + len(others)),
        out_specs=pl.BlockSpec(memory_space=pl.ANY),
        scratch_shapes=[
            pltpu.VMEM((count, width), jnp.bfloat16),
            pltpu.VMEM((rows, width), jnp.float32),
            pltpu.SemaphoreType.DMA((blocks,)),
        ],
        compiler_params=PARAMS,
        cost_estimate=cost(micros),
    )(scale, offset, raw, low, total, *others)


def exchange(value, target):
    count = lax.axis_size(AXES)
    return lax.ppermute(value, AXES, [(at, target(at) % count) for at in range(count)])


def partner(at):
    return at ^ 1


def onward(at):
    return at + 2 if at % 2 == 0 else at - 2


def backward(at):
    return at - 2 if at % 2 == 0 else at + 2


def tied(value, *others):
    return lax.optimization_barrier((value, *others))[0]


def shards(images, texts, logit_scale, logit_bias):
    rows = images.shape[0]
    args = (logit_scale, logit_bias)

    def cut(value, start, stop):
        return value[rows * start // 32 : rows * stop // 32]

    tail = cut(images, 24, 32)
    near0 = exchange(take_call(texts, rows * 16 // 32), partner)
    near1 = exchange(cut(texts, 16, 32), partner)
    side = exchange(tail, backward)
    img_low, txt_low, sum_img, sum_txt = own_call(*args, images, texts)
    far0 = exchange(tied(near0, img_low, side), onward)
    near2 = exchange(tied(cut(images, 0, 13), near0), partner)
    sum_img = add_call(*args, img_low, sum_img, (near0,), 0.8)
    far1 = exchange(tied(near1, sum_img), onward)
    near3 = exchange(tied(cut(images, 13, 24), near1), partner)
    sum_img = add_call(*args, img_low, sum_img, (near1,), 0.8)
    far2 = exchange(tied(near2, sum_img, far0), onward)
    near_tail = exchange(tied(tail, near2), partner)
    sum_txt = add_call(*args, txt_low, sum_txt, (near2,), 0.8)
    far3 = exchange(tied(near3, sum_txt, far1), onward)
    far_tail = exchange(tied(side, near3), partner)
    sum_txt = add_call(*args, txt_low, sum_txt, (near3,), 0.3)
    grad_img = last_call(*args, images, img_low, sum_img, (far0, far1,), 0.05)
    sum_txt = add_call(*args, txt_low, tied(sum_txt, far2, grad_img), (far2, near_tail,), 1.0)
    grad_txt = last_call(*args, texts, txt_low, sum_txt, (far3, far_tail), 0.05)
    return grad_img, grad_txt


def solution(mesh):
    split = P(AXES, None)
    return jax.shard_map(
        shards,
        mesh=mesh,
        in_specs=(split, split, P(), P()),
        out_specs=(split, split),
        check_vma=False,
    )
```

```python
import functools

import jax
import jax.numpy as jnp
from jax import lax
from jax.experimental import pallas as pl
from jax.experimental.pallas import tpu as pltpu
from jax.sharding import PartitionSpec as P

AXES = ("blk", "sub")
LAST = (((1,), (1,)), ((), ()))
FIRST = (((0,), (0,)), ((), ()))
VMEM_LIMIT = 24 * 1024 * 1024


def unit_rows(values_in):
    values = values_in.astype(jnp.float32)
    recip = lax.rsqrt(jnp.sum(values * values, axis=-1, keepdims=True) + 1e-06)
    return values * recip, recip


def dot32(left, right, dims):
    return lax.dot_general(left, right, dims, preferred_element_type=jnp.float32)


def band_term(own_low, other_low, scale, offset):
    weight = jax.nn.sigmoid(scale * dot32(own_low, other_low, LAST) + offset)
    return jnp.dot(
        weight.astype(jnp.bfloat16), other_low, preferred_element_type=jnp.float32
    )


def take_kernel(value_ref, out_ref, sem):
    copy = pltpu.make_async_copy(value_ref.at[pl.ds(0, out_ref.shape[0]), :], out_ref, sem)
    copy.start()
    copy.wait()


def own_kernel(scale_ref, offset_ref, img_ref, txt_ref, img_low, txt_low, sum_img, sum_txt):
    scale, offset = scale_ref[0], offset_ref[0]
    lower_rows((img_ref,), img_low)
    lower_rows((txt_ref,), txt_low)
    logits = scale * dot32(img_low[...], txt_low[...], LAST) + offset
    rows = lax.broadcasted_iota(jnp.int32, logits.shape, 0)
    columns = lax.broadcasted_iota(jnp.int32, logits.shape, 1)
    weight = jax.nn.sigmoid(logits) - (rows == columns).astype(jnp.float32)
    weight = weight.astype(jnp.bfloat16)
    sum_img[...] = jnp.dot(weight, txt_low[...], preferred_element_type=jnp.float32)
    sum_txt[...] = dot32(weight, img_low[...], FIRST)


def lower_rows(others, other_low):
    at = 0
    for other in others:
        rows = other.shape[0]
        other_low[at : at + rows, :] = unit_rows(other[...])[0].astype(jnp.bfloat16)
        at += rows


def add_kernel(count, scale_ref, offset_ref, low_ref, sum_in, *rest):
    others, (sum_out, other_low) = rest[:count], rest[count:]
    scale, offset = scale_ref[0], offset_ref[0]
    lower_rows(others, other_low)
    sum_out[...] = sum_in[...] + band_term(low_ref[...], other_low[...], scale, offset)


def last_kernel(count, blocks, scale_ref, offset_ref, raw_ref, low_ref, sum_ref, *rest):
    others, (out_ref, other_low, held, sems) = rest[:count], rest[count:]
    scale, offset = scale_ref[0], offset_ref[0]
    lower_rows(others, other_low)
    logits = scale * dot32(low_ref[...], other_low[...], LAST) + offset
    weight = jax.nn.sigmoid(logits).astype(jnp.bfloat16)
    size = held.shape[0] // blocks
    copies = []
    for block in range(blocks):
        start = block * size
        at = pl.ds(start, size)
        unit, recip = unit_rows(raw_ref[at, :])
        term = jnp.dot(
            weight[start : start + size], other_low[...], preferred_element_type=jnp.float32
        )
        grad = scale * (sum_ref[at, :] + term)
        along = jnp.sum(unit * grad, axis=-1, keepdims=True)
        held[at, :] = (grad - unit * along) * recip
        copy = pltpu.make_async_copy(held.at[at, :], out_ref.at[at, :], sems.at[block])
        copy.start()
        copies.append(copy)
    for copy in copies:
        copy.wait()


def cost(micros):
    return pl.CostEstimate(flops=int(micros * 1e9), bytes_accessed=1024, transcendentals=0)


SMEM = pl.BlockSpec(memory_space=pltpu.SMEM)
VMEM = pl.BlockSpec(memory_space=pltpu.VMEM)
PARAMS = pltpu.CompilerParams(vmem_limit_bytes=VMEM_LIMIT)


def take_call(value, count):
    return pl.pallas_call(
        take_kernel,
        out_shape=jax.ShapeDtypeStruct((count, value.shape[1]), value.dtype),
        in_specs=[pl.BlockSpec(memory_space=pl.ANY)],
        out_specs=VMEM,
        scratch_shapes=[pltpu.SemaphoreType.DMA],
        compiler_params=PARAMS,
        cost_estimate=cost(0.8),
    )(value)


def own_call(scale, offset, images, texts):
    rows, width = texts.shape
    low = jax.ShapeDtypeStruct((rows, width), jnp.bfloat16)
    total = jax.ShapeDtypeStruct((rows, width), jnp.float32)
    return pl.pallas_call(
        own_kernel,
        out_shape=(low, low, total, total),
        in_specs=[SMEM, SMEM, VMEM, VMEM],
        out_specs=(VMEM,) * 4,
        compiler_params=PARAMS,
        cost_estimate=cost(0.8),
    )(scale, offset, images, texts)


def add_call(scale, offset, low, total, others, micros):
    rows, width = low.shape
    count = sum(other.shape[0] for other in others)
    return pl.pallas_call(
        functools.partial(add_kernel, len(others)),
        out_shape=jax.ShapeDtypeStruct((rows, width), jnp.float32),
        in_specs=[SMEM, SMEM] + [VMEM] * (2 + len(others)),
        out_specs=VMEM,
        scratch_shapes=[pltpu.VMEM((count, width), jnp.bfloat16)],
        input_output_aliases={3: 0},
        compiler_params=PARAMS,
        cost_estimate=cost(micros),
    )(scale, offset, low, total, *others)


def last_call(scale, offset, raw, low, total, others, micros):
    rows, width = raw.shape
    count = sum(other.shape[0] for other in others)
    blocks = 4 if rows % 64 == 0 else 1
    return pl.pallas_call(
        functools.partial(last_kernel, len(others), blocks),
        out_shape=jax.ShapeDtypeStruct((rows, width), jnp.float32),
        in_specs=[SMEM, SMEM] + [VMEM] * (3 + len(others)),
        out_specs=pl.BlockSpec(memory_space=pl.ANY),
        scratch_shapes=[
            pltpu.VMEM((count, width), jnp.bfloat16),
            pltpu.VMEM((rows, width), jnp.float32),
            pltpu.SemaphoreType.DMA((blocks,)),
        ],
        compiler_params=PARAMS,
        cost_estimate=cost(micros),
    )(scale, offset, raw, low, total, *others)


def exchange(value, target):
    count = lax.axis_size(AXES)
    return lax.ppermute(value, AXES, [(at, target(at) % count) for at in range(count)])


def partner(at):
    return at ^ 1


def onward(at):
    return at + 2 if at % 2 == 0 else at - 2


def backward(at):
    return at - 2 if at % 2 == 0 else at + 2


def tied(value, *others):
    return lax.optimization_barrier((value, *others))[0]


def shards(images, texts, logit_scale, logit_bias):
    rows = images.shape[0]
    args = (logit_scale, logit_bias)

    def cut(value, start, stop):
        return value[rows * start // 32 : rows * stop // 32]

    tail = cut(images, 21, 32)
    lead = take_call(texts, rows * 16 // 32)
    near0 = exchange(lead, partner)
    near1 = exchange(tied(cut(texts, 16, 32), lead), partner)
    side = exchange(tail, backward)
    img_low, txt_low, sum_img, sum_txt = own_call(*args, images, texts)
    far0 = exchange(tied(near0, img_low), onward)
    near2 = exchange(tied(cut(images, 0, 11), near0), partner)
    sum_img = add_call(*args, img_low, tied(sum_img, side), (near0,), 0.8)
    far1 = exchange(tied(near1, sum_img), onward)
    near3 = exchange(tied(cut(images, 11, 21), near1), partner)
    sum_img = add_call(*args, img_low, sum_img, (near1,), 0.8)
    far2 = exchange(tied(near2, sum_img, far0), onward)
    near_tail = exchange(tied(tail, near2), partner)
    far_tail = exchange(tied(side, near2), partner)
    sum_txt = add_call(*args, txt_low, sum_txt, (near2,), 0.8)
    far3 = exchange(tied(near3, sum_txt, far1), onward)
    grad_img = last_call(*args, images, img_low, sum_img, (far0, far1,), 0.05)
    sum_txt = add_call(*args, txt_low, tied(sum_txt, grad_img), (near3, far2,), 0.8)
    sum_txt = add_call(*args, txt_low, sum_txt, (near_tail,), 1.0)
    sum_txt = add_call(*args, txt_low, sum_txt, (far_tail,), 0.05)
    grad_txt = last_call(*args, texts, txt_low, sum_txt, (far3,), 0.05)
    return grad_img, grad_txt


def solution(mesh):
    split = P(AXES, None)
    return jax.shard_map(
        shards,
        mesh=mesh,
        in_specs=(split, split, P(), P()),
        out_specs=(split, split),
        check_vma=False,
    )
```

```python
import functools

import jax
import jax.numpy as jnp
from jax import lax
from jax.experimental import pallas as pl
from jax.experimental.pallas import tpu as pltpu
from jax.sharding import PartitionSpec as P

AXES = ("blk", "sub")
LAST = (((1,), (1,)), ((), ()))
FIRST = (((0,), (0,)), ((), ()))
VMEM_LIMIT = 24 * 1024 * 1024


def unit_rows(values_in):
    values = values_in.astype(jnp.float32)
    recip = lax.rsqrt(jnp.sum(values * values, axis=-1, keepdims=True) + 1e-06)
    return values * recip, recip


def dot32(left, right, dims):
    return lax.dot_general(left, right, dims, preferred_element_type=jnp.float32)


def band_term(own_low, other_low, scale, offset):
    weight = jax.nn.sigmoid(scale * dot32(own_low, other_low, LAST) + offset)
    return jnp.dot(
        weight.astype(jnp.bfloat16), other_low, preferred_element_type=jnp.float32
    )


def take_kernel(value_ref, out_ref, sem):
    copy = pltpu.make_async_copy(value_ref.at[pl.ds(0, out_ref.shape[0]), :], out_ref, sem)
    copy.start()
    copy.wait()


def own_kernel(scale_ref, offset_ref, img_ref, txt_ref, img_low, txt_low, sum_img, sum_txt):
    scale, offset = scale_ref[0], offset_ref[0]
    lower_rows((img_ref,), img_low)
    lower_rows((txt_ref,), txt_low)
    logits = scale * dot32(img_low[...], txt_low[...], LAST) + offset
    rows = lax.broadcasted_iota(jnp.int32, logits.shape, 0)
    columns = lax.broadcasted_iota(jnp.int32, logits.shape, 1)
    weight = jax.nn.sigmoid(logits) - (rows == columns).astype(jnp.float32)
    weight = weight.astype(jnp.bfloat16)
    sum_img[...] = jnp.dot(weight, txt_low[...], preferred_element_type=jnp.float32)
    sum_txt[...] = dot32(weight, img_low[...], FIRST)


def lower_rows(others, other_low):
    at = 0
    for other in others:
        rows = other.shape[0]
        other_low[at : at + rows, :] = unit_rows(other[...])[0].astype(jnp.bfloat16)
        at += rows


def add_kernel(count, scale_ref, offset_ref, low_ref, sum_in, *rest):
    others, (sum_out, other_low) = rest[:count], rest[count:]
    scale, offset = scale_ref[0], offset_ref[0]
    lower_rows(others, other_low)
    sum_out[...] = sum_in[...] + band_term(low_ref[...], other_low[...], scale, offset)


def last_kernel(count, blocks, scale_ref, offset_ref, raw_ref, low_ref, sum_ref, *rest):
    others, (out_ref, other_low, held, sems) = rest[:count], rest[count:]
    scale, offset = scale_ref[0], offset_ref[0]
    lower_rows(others, other_low)
    logits = scale * dot32(low_ref[...], other_low[...], LAST) + offset
    weight = jax.nn.sigmoid(logits).astype(jnp.bfloat16)
    size = held.shape[0] // blocks
    copies = []
    for block in range(blocks):
        start = block * size
        at = pl.ds(start, size)
        unit, recip = unit_rows(raw_ref[at, :])
        term = jnp.dot(
            weight[start : start + size], other_low[...], preferred_element_type=jnp.float32
        )
        grad = scale * (sum_ref[at, :] + term)
        along = jnp.sum(unit * grad, axis=-1, keepdims=True)
        held[at, :] = (grad - unit * along) * recip
        copy = pltpu.make_async_copy(held.at[at, :], out_ref.at[at, :], sems.at[block])
        copy.start()
        copies.append(copy)
    for copy in copies:
        copy.wait()


def cost(micros):
    return pl.CostEstimate(flops=int(micros * 1e9), bytes_accessed=1024, transcendentals=0)


SMEM = pl.BlockSpec(memory_space=pltpu.SMEM)
VMEM = pl.BlockSpec(memory_space=pltpu.VMEM)
PARAMS = pltpu.CompilerParams(vmem_limit_bytes=VMEM_LIMIT)


def take_call(value, count):
    return pl.pallas_call(
        take_kernel,
        out_shape=jax.ShapeDtypeStruct((count, value.shape[1]), value.dtype),
        in_specs=[pl.BlockSpec(memory_space=pl.ANY)],
        out_specs=VMEM,
        scratch_shapes=[pltpu.SemaphoreType.DMA],
        compiler_params=PARAMS,
        cost_estimate=cost(0.8),
    )(value)


def own_call(scale, offset, images, texts):
    rows, width = texts.shape
    low = jax.ShapeDtypeStruct((rows, width), jnp.bfloat16)
    total = jax.ShapeDtypeStruct((rows, width), jnp.float32)
    return pl.pallas_call(
        own_kernel,
        out_shape=(low, low, total, total),
        in_specs=[SMEM, SMEM, VMEM, VMEM],
        out_specs=(VMEM,) * 4,
        compiler_params=PARAMS,
        cost_estimate=cost(0.8),
    )(scale, offset, images, texts)


def add_call(scale, offset, low, total, others, micros):
    rows, width = low.shape
    count = sum(other.shape[0] for other in others)
    return pl.pallas_call(
        functools.partial(add_kernel, len(others)),
        out_shape=jax.ShapeDtypeStruct((rows, width), jnp.float32),
        in_specs=[SMEM, SMEM] + [VMEM] * (2 + len(others)),
        out_specs=VMEM,
        scratch_shapes=[pltpu.VMEM((count, width), jnp.bfloat16)],
        input_output_aliases={3: 0},
        compiler_params=PARAMS,
        cost_estimate=cost(micros),
    )(scale, offset, low, total, *others)


def last_call(scale, offset, raw, low, total, others, micros):
    rows, width = raw.shape
    count = sum(other.shape[0] for other in others)
    blocks = 4 if rows % 64 == 0 else 1
    return pl.pallas_call(
        functools.partial(last_kernel, len(others), blocks),
        out_shape=jax.ShapeDtypeStruct((rows, width), jnp.float32),
        in_specs=[SMEM, SMEM] + [VMEM] * (3 + len(others)),
        out_specs=pl.BlockSpec(memory_space=pl.ANY),
        scratch_shapes=[
            pltpu.VMEM((count, width), jnp.bfloat16),
            pltpu.VMEM((rows, width), jnp.float32),
            pltpu.SemaphoreType.DMA((blocks,)),
        ],
        compiler_params=PARAMS,
        cost_estimate=cost(micros),
    )(scale, offset, raw, low, total, *others)


def exchange(value, target):
    count = lax.axis_size(AXES)
    return lax.ppermute(value, AXES, [(at, target(at) % count) for at in range(count)])


def partner(at):
    return at ^ 1


def onward(at):
    return at + 2 if at % 2 == 0 else at - 2


def backward(at):
    return at - 2 if at % 2 == 0 else at + 2


def tied(value, *others):
    return lax.optimization_barrier((value, *others))[0]


def shards(images, texts, logit_scale, logit_bias):
    rows = images.shape[0]
    args = (logit_scale, logit_bias)

    def cut(value, start, stop):
        return value[rows * start // 32 : rows * stop // 32]

    tail = cut(images, 22, 32)
    lead = take_call(texts, rows * 11 // 32)
    near0 = exchange(lead, partner)
    near1 = exchange(tied(cut(texts, 11, 21), lead), partner)
    near2 = exchange(tied(cut(texts, 21, 32), lead), partner)
    near3 = exchange(tied(cut(images, 0, 11), lead), partner)
    side = exchange(tail, backward)
    img_low, txt_low, sum_img, sum_txt = own_call(*args, images, texts)
    far0 = exchange(near0, onward)
    near4 = exchange(tied(cut(images, 11, 22), near0), partner)
    far1 = exchange(tied(near1, img_low), onward)
    near_tail = exchange(tied(tail, near1), partner)
    far_tail = exchange(tied(side, near1), partner)
    sum_img = add_call(*args, img_low, tied(sum_img, side), (near1, near0,), 0.4)
    far2 = exchange(tied(near2, sum_img, far0), onward)
    sum_img = add_call(*args, img_low, sum_img, (near2,), 0.4)
    far3 = exchange(tied(near3, sum_img, far1), onward)
    sum_txt = add_call(*args, txt_low, sum_txt, (near3,), 0.4)
    far4 = exchange(tied(near4, sum_txt), onward)
    grad_img = last_call(*args, images, img_low, sum_img, (far0, far1, far2,), 0.05)
    sum_txt = add_call(*args, txt_low, tied(sum_txt, grad_img), (near4, far3,), 0.4)
    sum_txt = add_call(*args, txt_low, sum_txt, (near_tail,), 1.0)
    grad_txt = last_call(*args, texts, txt_low, sum_txt, (far4, far_tail), 0.05)
    return grad_img, grad_txt


def solution(mesh):
    split = P(AXES, None)
    return jax.shard_map(
        shards,
        mesh=mesh,
        in_specs=(split, split, P(), P()),
        out_specs=(split, split),
        check_vma=False,
    )
```

```python
import functools

import jax
import jax.numpy as jnp
from jax import lax
from jax.experimental import pallas as pl
from jax.experimental.pallas import tpu as pltpu
from jax.sharding import PartitionSpec as P

AXES = ("blk", "sub")
LAST = (((1,), (1,)), ((), ()))
FIRST = (((0,), (0,)), ((), ()))
VMEM_LIMIT = 24 * 1024 * 1024


def unit_rows(values_in):
    values = values_in.astype(jnp.float32)
    recip = lax.rsqrt(jnp.sum(values * values, axis=-1, keepdims=True) + 1e-06)
    return values * recip, recip


def dot32(left, right, dims):
    return lax.dot_general(left, right, dims, preferred_element_type=jnp.float32)


def band_term(own_low, other_low, scale, offset):
    weight = jax.nn.sigmoid(scale * dot32(own_low, other_low, LAST) + offset)
    return jnp.dot(
        weight.astype(jnp.bfloat16), other_low, preferred_element_type=jnp.float32
    )


def take_kernel(value_ref, out_ref, sem):
    copy = pltpu.make_async_copy(value_ref.at[pl.ds(0, out_ref.shape[0]), :], out_ref, sem)
    copy.start()
    copy.wait()


def own_kernel(scale_ref, offset_ref, img_ref, txt_ref, img_low, txt_low, sum_img, sum_txt):
    scale, offset = scale_ref[0], offset_ref[0]
    lower_rows((img_ref,), img_low)
    lower_rows((txt_ref,), txt_low)
    logits = scale * dot32(img_low[...], txt_low[...], LAST) + offset
    rows = lax.broadcasted_iota(jnp.int32, logits.shape, 0)
    columns = lax.broadcasted_iota(jnp.int32, logits.shape, 1)
    weight = jax.nn.sigmoid(logits) - (rows == columns).astype(jnp.float32)
    weight = weight.astype(jnp.bfloat16)
    sum_img[...] = jnp.dot(weight, txt_low[...], preferred_element_type=jnp.float32)
    sum_txt[...] = dot32(weight, img_low[...], FIRST)


def lower_rows(others, other_low):
    at = 0
    for other in others:
        rows = other.shape[0]
        other_low[at : at + rows, :] = unit_rows(other[...])[0].astype(jnp.bfloat16)
        at += rows


def add_kernel(count, scale_ref, offset_ref, low_ref, sum_in, *rest):
    others, (sum_out, other_low) = rest[:count], rest[count:]
    scale, offset = scale_ref[0], offset_ref[0]
    lower_rows(others, other_low)
    sum_out[...] = sum_in[...] + band_term(low_ref[...], other_low[...], scale, offset)


def unit_kernel(value_ref, unit_ref, recip_ref):
    unit_ref[...], recip_ref[...] = unit_rows(value_ref[...])


def low_kernel(value_ref, low_ref):
    low_ref[...] = unit_rows(value_ref[...])[0].astype(jnp.bfloat16)


def last_kernel(count, raw_count, blocks, scale_ref, offset_ref, unit_ref, recip_ref, low_ref, sum_ref, *rest):
    others, (out_ref, other_low, held, sems) = rest[:count], rest[count:]
    scale, offset = scale_ref[0], offset_ref[0]
    lower_rows(others[:raw_count], other_low)
    if count > raw_count:
        at = sum(other.shape[0] for other in others[:raw_count])
        other_low[at:, :] = others[-1][...]
    logits = scale * dot32(low_ref[...], other_low[...], LAST) + offset
    weight = jax.nn.sigmoid(logits).astype(jnp.bfloat16)
    size = held.shape[0] // blocks
    copies = []
    for block in range(blocks):
        start = block * size
        at = pl.ds(start, size)
        unit = unit_ref[at, :]
        term = jnp.dot(
            weight[start : start + size], other_low[...], preferred_element_type=jnp.float32
        )
        grad = scale * (sum_ref[at, :] + term)
        along = jnp.sum(unit * grad, axis=-1, keepdims=True)
        held[at, :] = (grad - unit * along) * recip_ref[at, :]
        copy = pltpu.make_async_copy(held.at[at, :], out_ref.at[at, :], sems.at[block])
        copy.start()
        copies.append(copy)
    for copy in copies:
        copy.wait()


def cost(micros):
    return pl.CostEstimate(flops=int(micros * 1e9), bytes_accessed=1024, transcendentals=0)


SMEM = pl.BlockSpec(memory_space=pltpu.SMEM)
VMEM = pl.BlockSpec(memory_space=pltpu.VMEM)
PARAMS = pltpu.CompilerParams(vmem_limit_bytes=VMEM_LIMIT)


def take_call(value, count):
    return pl.pallas_call(
        take_kernel,
        out_shape=jax.ShapeDtypeStruct((count, value.shape[1]), value.dtype),
        in_specs=[pl.BlockSpec(memory_space=pl.ANY)],
        out_specs=VMEM,
        scratch_shapes=[pltpu.SemaphoreType.DMA],
        compiler_params=PARAMS,
        cost_estimate=cost(0.8),
    )(value)


def own_call(scale, offset, images, texts):
    rows, width = texts.shape
    low = jax.ShapeDtypeStruct((rows, width), jnp.bfloat16)
    total = jax.ShapeDtypeStruct((rows, width), jnp.float32)
    return pl.pallas_call(
        own_kernel,
        out_shape=(low, low, total, total),
        in_specs=[SMEM, SMEM, VMEM, VMEM],
        out_specs=(VMEM,) * 4,
        compiler_params=PARAMS,
        cost_estimate=cost(0.8),
    )(scale, offset, images, texts)


def add_call(scale, offset, low, total, others, micros):
    rows, width = low.shape
    count = sum(other.shape[0] for other in others)
    return pl.pallas_call(
        functools.partial(add_kernel, len(others)),
        out_shape=jax.ShapeDtypeStruct((rows, width), jnp.float32),
        in_specs=[SMEM, SMEM] + [VMEM] * (2 + len(others)),
        out_specs=VMEM,
        scratch_shapes=[pltpu.VMEM((count, width), jnp.bfloat16)],
        input_output_aliases={3: 0},
        compiler_params=PARAMS,
        cost_estimate=cost(micros),
    )(scale, offset, low, total, *others)


def last_call(scale, offset, unit, recip, low, total, others, raw_count, micros):
    rows, width = unit.shape
    count = sum(other.shape[0] for other in others)
    blocks = 4 if rows % 64 == 0 else 1
    return pl.pallas_call(
        functools.partial(last_kernel, len(others), raw_count, blocks),
        out_shape=jax.ShapeDtypeStruct((rows, width), jnp.float32),
        in_specs=[SMEM, SMEM] + [VMEM] * (4 + len(others)),
        out_specs=pl.BlockSpec(memory_space=pl.ANY),
        scratch_shapes=[
            pltpu.VMEM((count, width), jnp.bfloat16),
            pltpu.VMEM((rows, width), jnp.float32),
            pltpu.SemaphoreType.DMA((blocks,)),
        ],
        compiler_params=PARAMS,
        cost_estimate=cost(micros),
    )(scale, offset, unit, recip, low, total, *others)


def unit_call(value):
    rows, width = value.shape
    return pl.pallas_call(
        unit_kernel,
        out_shape=(
            jax.ShapeDtypeStruct((rows, width), jnp.float32),
            jax.ShapeDtypeStruct((rows, 1), jnp.float32),
        ),
        in_specs=[VMEM],
        out_specs=(VMEM, VMEM),
        compiler_params=PARAMS,
        cost_estimate=cost(0.05),
    )(value)


def low_call(value):
    return pl.pallas_call(
        low_kernel,
        out_shape=jax.ShapeDtypeStruct(value.shape, jnp.bfloat16),
        in_specs=[VMEM],
        out_specs=VMEM,
        compiler_params=PARAMS,
        cost_estimate=cost(0.3),
    )(value)


def exchange(value, target):
    count = lax.axis_size(AXES)
    return lax.ppermute(value, AXES, [(at, target(at) % count) for at in range(count)])


def partner(at):
    return at ^ 1


def onward(at):
    return at + 2 if at % 2 == 0 else at - 2


def backward(at):
    return at - 2 if at % 2 == 0 else at + 2


def tied(value, *others):
    return lax.optimization_barrier((value, *others))[0]


def shards(images, texts, logit_scale, logit_bias):
    rows = images.shape[0]
    args = (logit_scale, logit_bias)

    def cut(value, start, stop):
        return value[rows * start // 32 : rows * stop // 32]

    tail = cut(images, 22, 32)
    lead = take_call(texts, rows * 11 // 32)
    near0 = exchange(lead, partner)
    near1 = exchange(tied(cut(texts, 11, 21), lead), partner)
    near2 = exchange(tied(cut(texts, 21, 32), lead), partner)
    near3 = exchange(tied(cut(images, 0, 11), lead), partner)
    side = exchange(tail, backward)
    img_low, txt_low, sum_img, sum_txt = own_call(*args, images, texts)
    far0 = exchange(near0, onward)
    near4 = exchange(tied(cut(images, 11, 22), near0), partner)
    far1 = exchange(tied(near1, img_low), onward)
    near_tail = exchange(tied(tail, near1), partner)
    far_tail = exchange(tied(side, near1), partner)
    sum_img = add_call(*args, img_low, tied(sum_img, side), (near1, near0,), 0.4)
    far2 = exchange(tied(near2, sum_img, far0), onward)
    sum_img = add_call(*args, img_low, sum_img, (near2,), 0.4)
    unit_img, recip_img = unit_call(tied(images, sum_img))
    unit_txt, recip_txt = unit_call(tied(texts, unit_img))
    far3 = exchange(tied(near3, unit_txt, unit_img, sum_img, far1), onward)
    sum_txt = add_call(*args, txt_low, sum_txt, (near3,), 0.4)
    far4 = exchange(tied(near4, sum_txt), onward)
    grad_img = last_call(*args, unit_img, recip_img, img_low, sum_img, (far0, far1, far2), 3, 0.05)
    sum_txt = add_call(*args, txt_low, tied(sum_txt, grad_img), (near4, far3,), 0.4)
    sum_txt = add_call(*args, txt_low, sum_txt, (near_tail,), 1.0)
    grad_txt = last_call(*args, unit_txt, recip_txt, txt_low, sum_txt, (far4, low_call(tied(far_tail, sum_txt))), 1, 0.05)
    return grad_img, grad_txt


def solution(mesh):
    split = P(AXES, None)
    return jax.shard_map(
        shards,
        mesh=mesh,
        in_specs=(split, split, P(), P()),
        out_specs=(split, split),
        check_vma=False,
    )
```

```python
import functools

import jax
import jax.numpy as jnp
from jax import lax
from jax.experimental import pallas as pl
from jax.experimental.pallas import tpu as pltpu
from jax.sharding import PartitionSpec as P

AXES = ("blk", "sub")
LAST = (((1,), (1,)), ((), ()))
FIRST = (((0,), (0,)), ((), ()))
VMEM_LIMIT = 24 * 1024 * 1024


def unit_rows(values_in):
    values = values_in.astype(jnp.float32)
    recip = lax.rsqrt(jnp.sum(values * values, axis=-1, keepdims=True) + 1e-06)
    return values * recip, recip


def dot32(left, right, dims):
    return lax.dot_general(left, right, dims, preferred_element_type=jnp.float32)


def band_term(own_low, other_low, scale, offset):
    weight = jax.nn.sigmoid(scale * dot32(own_low, other_low, LAST) + offset)
    return jnp.dot(
        weight.astype(jnp.bfloat16), other_low, preferred_element_type=jnp.float32
    )


def take_kernel(value_ref, out_ref, sem):
    copy = pltpu.make_async_copy(value_ref.at[pl.ds(0, out_ref.shape[0]), :], out_ref, sem)
    copy.start()
    copy.wait()


def own_kernel(scale_ref, offset_ref, img_ref, txt_ref, img_low, txt_low, sum_img, sum_txt):
    scale, offset = scale_ref[0], offset_ref[0]
    lower_rows((img_ref,), img_low)
    lower_rows((txt_ref,), txt_low)
    logits = scale * dot32(img_low[...], txt_low[...], LAST) + offset
    rows = lax.broadcasted_iota(jnp.int32, logits.shape, 0)
    columns = lax.broadcasted_iota(jnp.int32, logits.shape, 1)
    weight = jax.nn.sigmoid(logits) - (rows == columns).astype(jnp.float32)
    weight = weight.astype(jnp.bfloat16)
    sum_img[...] = jnp.dot(weight, txt_low[...], preferred_element_type=jnp.float32)
    sum_txt[...] = dot32(weight, img_low[...], FIRST)


def lower_rows(others, other_low):
    at = 0
    for other in others:
        rows = other.shape[0]
        other_low[at : at + rows, :] = unit_rows(other[...])[0].astype(jnp.bfloat16)
        at += rows


def add_kernel(count, scale_ref, offset_ref, low_ref, sum_in, *rest):
    others, (sum_out, other_low) = rest[:count], rest[count:]
    scale, offset = scale_ref[0], offset_ref[0]
    lower_rows(others, other_low)
    sum_out[...] = sum_in[...] + band_term(low_ref[...], other_low[...], scale, offset)


def unit_kernel(value_ref, unit_ref, recip_ref):
    unit_ref[...], recip_ref[...] = unit_rows(value_ref[...])


def low_kernel(value_ref, low_ref):
    low_ref[...] = unit_rows(value_ref[...])[0].astype(jnp.bfloat16)


def last_kernel(count, raw_count, blocks, scale_ref, offset_ref, unit_ref, recip_ref, low_ref, sum_ref, *rest):
    others, (out_ref, other_low, held, sems) = rest[:count], rest[count:]
    scale, offset = scale_ref[0], offset_ref[0]
    lower_rows(others[:raw_count], other_low)
    if count > raw_count:
        at = sum(other.shape[0] for other in others[:raw_count])
        other_low[at:, :] = others[-1][...]
    logits = scale * dot32(low_ref[...], other_low[...], LAST) + offset
    weight = jax.nn.sigmoid(logits).astype(jnp.bfloat16)
    size = held.shape[0] // blocks
    copies = []
    for block in range(blocks):
        start = block * size
        at = pl.ds(start, size)
        unit = unit_ref[at, :]
        term = jnp.dot(
            weight[start : start + size], other_low[...], preferred_element_type=jnp.float32
        )
        grad = scale * (sum_ref[at, :] + term)
        along = jnp.sum(unit * grad, axis=-1, keepdims=True)
        held[at, :] = (grad - unit * along) * recip_ref[at, :]
        copy = pltpu.make_async_copy(held.at[at, :], out_ref.at[at, :], sems.at[block])
        copy.start()
        copies.append(copy)
    for copy in copies:
        copy.wait()


def cost(micros):
    return pl.CostEstimate(flops=int(micros * 1e9), bytes_accessed=1024, transcendentals=0)


SMEM = pl.BlockSpec(memory_space=pltpu.SMEM)
VMEM = pl.BlockSpec(memory_space=pltpu.VMEM)
PARAMS = pltpu.CompilerParams(vmem_limit_bytes=VMEM_LIMIT)


def take_call(value, count):
    return pl.pallas_call(
        take_kernel,
        out_shape=jax.ShapeDtypeStruct((count, value.shape[1]), value.dtype),
        in_specs=[pl.BlockSpec(memory_space=pl.ANY)],
        out_specs=VMEM,
        scratch_shapes=[pltpu.SemaphoreType.DMA],
        compiler_params=PARAMS,
        cost_estimate=cost(0.8),
    )(value)


def own_call(scale, offset, images, texts):
    rows, width = texts.shape
    low = jax.ShapeDtypeStruct((rows, width), jnp.bfloat16)
    total = jax.ShapeDtypeStruct((rows, width), jnp.float32)
    return pl.pallas_call(
        own_kernel,
        out_shape=(low, low, total, total),
        in_specs=[SMEM, SMEM, VMEM, VMEM],
        out_specs=(VMEM,) * 4,
        compiler_params=PARAMS,
        cost_estimate=cost(0.8),
    )(scale, offset, images, texts)


def add_call(scale, offset, low, total, others, micros):
    rows, width = low.shape
    count = sum(other.shape[0] for other in others)
    return pl.pallas_call(
        functools.partial(add_kernel, len(others)),
        out_shape=jax.ShapeDtypeStruct((rows, width), jnp.float32),
        in_specs=[SMEM, SMEM] + [VMEM] * (2 + len(others)),
        out_specs=VMEM,
        scratch_shapes=[pltpu.VMEM((count, width), jnp.bfloat16)],
        input_output_aliases={3: 0},
        compiler_params=PARAMS,
        cost_estimate=cost(micros),
    )(scale, offset, low, total, *others)


def last_call(scale, offset, unit, recip, low, total, others, raw_count, micros):
    rows, width = unit.shape
    count = sum(other.shape[0] for other in others)
    blocks = 4 if rows % 64 == 0 else 1
    return pl.pallas_call(
        functools.partial(last_kernel, len(others), raw_count, blocks),
        out_shape=jax.ShapeDtypeStruct((rows, width), jnp.float32),
        in_specs=[SMEM, SMEM] + [VMEM] * (4 + len(others)),
        out_specs=pl.BlockSpec(memory_space=pl.ANY),
        scratch_shapes=[
            pltpu.VMEM((count, width), jnp.bfloat16),
            pltpu.VMEM((rows, width), jnp.float32),
            pltpu.SemaphoreType.DMA((blocks,)),
        ],
        compiler_params=PARAMS,
        cost_estimate=cost(micros),
    )(scale, offset, unit, recip, low, total, *others)


def unit_call(value):
    rows, width = value.shape
    return pl.pallas_call(
        unit_kernel,
        out_shape=(
            jax.ShapeDtypeStruct((rows, width), jnp.float32),
            jax.ShapeDtypeStruct((rows, 1), jnp.float32),
        ),
        in_specs=[VMEM],
        out_specs=(VMEM, VMEM),
        compiler_params=PARAMS,
        cost_estimate=cost(0.05),
    )(value)


def low_call(value):
    return pl.pallas_call(
        low_kernel,
        out_shape=jax.ShapeDtypeStruct(value.shape, jnp.bfloat16),
        in_specs=[VMEM],
        out_specs=VMEM,
        compiler_params=PARAMS,
        cost_estimate=cost(0.3),
    )(value)


def exchange(value, target):
    count = lax.axis_size(AXES)
    return lax.ppermute(value, AXES, [(at, target(at) % count) for at in range(count)])


def partner(at):
    return at ^ 1


def onward(at):
    return at + 2 if at % 2 == 0 else at - 2


def backward(at):
    return at - 2 if at % 2 == 0 else at + 2


def tied(value, *others):
    return lax.optimization_barrier((value, *others))[0]


def shards(images, texts, logit_scale, logit_bias):
    rows = images.shape[0]
    args = (logit_scale, logit_bias)

    def cut(value, start, stop):
        return value[rows * start // 32 : rows * stop // 32]

    tail = cut(images, 22, 32)
    lead = take_call(texts, rows * 11 // 32)
    near0 = exchange(lead, partner)
    near1 = exchange(tied(cut(texts, 11, 21), lead), partner)
    near2 = exchange(tied(cut(texts, 21, 32), lead), partner)
    near3 = exchange(tied(cut(images, 0, 11), lead), partner)
    side = exchange(tail, backward)
    img_low, txt_low, sum_img, sum_txt = own_call(*args, images, texts)
    far0 = exchange(near0, onward)
    near4 = exchange(tied(cut(images, 11, 22), near0), partner)
    far1 = exchange(tied(near1, img_low), onward)
    near_tail = exchange(tied(tail, near1), partner)
    far_tail = exchange(tied(side, near1), partner)
    sum_img = add_call(*args, img_low, tied(sum_img, side), (near1, near0,), 0.2)
    far2 = exchange(tied(near2, sum_img, far0), onward)
    sum_img = add_call(*args, img_low, sum_img, (near2,), 0.2)
    unit_img, recip_img = unit_call(tied(images, sum_img))
    unit_txt, recip_txt = unit_call(tied(texts, unit_img))
    far3 = exchange(tied(near3, unit_txt, unit_img, sum_img, far1), onward)
    sum_txt = add_call(*args, txt_low, sum_txt, (near3,), 0.2)
    far4 = exchange(tied(near4, sum_txt), onward)
    grad_img = last_call(*args, unit_img, recip_img, img_low, sum_img, (far0, far1, far2), 3, 0.05)
    sum_txt = add_call(*args, txt_low, tied(sum_txt, grad_img), (near_tail,), 0.3)
    sum_txt = add_call(*args, txt_low, sum_txt, (near4, far3,), 0.2)
    grad_txt = last_call(*args, unit_txt, recip_txt, txt_low, sum_txt, (far4, low_call(tied(far_tail, sum_txt))), 1, 0.05)
    return grad_img, grad_txt


def solution(mesh):
    split = P(AXES, None)
    return jax.shard_map(
        shards,
        mesh=mesh,
        in_specs=(split, split, P(), P()),
        out_specs=(split, split),
        check_vma=False,
    )
```

```python
import functools

import jax
import jax.numpy as jnp
from jax import lax
from jax.experimental import pallas as pl
from jax.experimental.pallas import tpu as pltpu
from jax.sharding import PartitionSpec as P

AXES = ("blk", "sub")
LAST = (((1,), (1,)), ((), ()))
FIRST = (((0,), (0,)), ((), ()))
VMEM_LIMIT = 24 * 1024 * 1024


def unit_rows(values_in):
    values = values_in.astype(jnp.float32)
    recip = lax.rsqrt(jnp.sum(values * values, axis=-1, keepdims=True) + 1e-06)
    return values * recip, recip


def dot32(left, right, dims):
    return lax.dot_general(left, right, dims, preferred_element_type=jnp.float32)


def band_term(own_low, other_low, scale, offset):
    weight = jax.nn.sigmoid(scale * dot32(own_low, other_low, LAST) + offset)
    return jnp.dot(
        weight.astype(jnp.bfloat16), other_low, preferred_element_type=jnp.float32
    )


def take_kernel(value_ref, out_ref, sem):
    copy = pltpu.make_async_copy(value_ref.at[pl.ds(0, out_ref.shape[0]), :], out_ref, sem)
    copy.start()
    copy.wait()


def own_kernel(scale_ref, offset_ref, img_ref, txt_ref, img_low, txt_low, sum_img, sum_txt):
    scale, offset = scale_ref[0], offset_ref[0]
    lower_rows((img_ref,), img_low)
    lower_rows((txt_ref,), txt_low)
    logits = scale * dot32(img_low[...], txt_low[...], LAST) + offset
    rows = lax.broadcasted_iota(jnp.int32, logits.shape, 0)
    columns = lax.broadcasted_iota(jnp.int32, logits.shape, 1)
    weight = jax.nn.sigmoid(logits) - (rows == columns).astype(jnp.float32)
    weight = weight.astype(jnp.bfloat16)
    sum_img[...] = jnp.dot(weight, txt_low[...], preferred_element_type=jnp.float32)
    sum_txt[...] = dot32(weight, img_low[...], FIRST)


def lower_rows(others, other_low):
    at = 0
    for other in others:
        rows = other.shape[0]
        other_low[at : at + rows, :] = unit_rows(other[...])[0].astype(jnp.bfloat16)
        at += rows


def add_kernel(count, scale_ref, offset_ref, low_ref, sum_in, *rest):
    others, (sum_out, other_low) = rest[:count], rest[count:]
    scale, offset = scale_ref[0], offset_ref[0]
    lower_rows(others, other_low)
    sum_out[...] = sum_in[...] + band_term(low_ref[...], other_low[...], scale, offset)


def unit_kernel(value_ref, unit_ref, recip_ref):
    unit_ref[...], recip_ref[...] = unit_rows(value_ref[...])


def last_kernel(count, blocks, scale_ref, offset_ref, unit_ref, recip_ref, low_ref, sum_ref, *rest):
    others, (out_ref, other_low, held, sems) = rest[:count], rest[count:]
    scale, offset = scale_ref[0], offset_ref[0]
    lower_rows(others, other_low)
    logits = scale * dot32(low_ref[...], other_low[...], LAST) + offset
    weight = jax.nn.sigmoid(logits).astype(jnp.bfloat16)
    size = held.shape[0] // blocks
    copies = []
    for block in range(blocks):
        start = block * size
        at = pl.ds(start, size)
        unit = unit_ref[at, :]
        term = jnp.dot(
            weight[start : start + size], other_low[...], preferred_element_type=jnp.float32
        )
        grad = scale * (sum_ref[at, :] + term)
        along = jnp.sum(unit * grad, axis=-1, keepdims=True)
        held[at, :] = (grad - unit * along) * recip_ref[at, :]
        copy = pltpu.make_async_copy(held.at[at, :], out_ref.at[at, :], sems.at[block])
        copy.start()
        copies.append(copy)
    for copy in copies:
        copy.wait()


def cost(micros):
    return pl.CostEstimate(flops=int(micros * 1e9), bytes_accessed=1024, transcendentals=0)


SMEM = pl.BlockSpec(memory_space=pltpu.SMEM)
VMEM = pl.BlockSpec(memory_space=pltpu.VMEM)
PARAMS = pltpu.CompilerParams(vmem_limit_bytes=VMEM_LIMIT)


def take_call(value, count):
    return pl.pallas_call(
        take_kernel,
        out_shape=jax.ShapeDtypeStruct((count, value.shape[1]), value.dtype),
        in_specs=[pl.BlockSpec(memory_space=pl.ANY)],
        out_specs=VMEM,
        scratch_shapes=[pltpu.SemaphoreType.DMA],
        compiler_params=PARAMS,
        cost_estimate=cost(0.8),
    )(value)


def own_call(scale, offset, images, texts):
    rows, width = texts.shape
    low = jax.ShapeDtypeStruct((rows, width), jnp.bfloat16)
    total = jax.ShapeDtypeStruct((rows, width), jnp.float32)
    return pl.pallas_call(
        own_kernel,
        out_shape=(low, low, total, total),
        in_specs=[SMEM, SMEM, VMEM, VMEM],
        out_specs=(VMEM,) * 4,
        compiler_params=PARAMS,
        cost_estimate=cost(0.8),
    )(scale, offset, images, texts)


def add_call(scale, offset, low, total, others, micros):
    rows, width = low.shape
    count = sum(other.shape[0] for other in others)
    return pl.pallas_call(
        functools.partial(add_kernel, len(others)),
        out_shape=jax.ShapeDtypeStruct((rows, width), jnp.float32),
        in_specs=[SMEM, SMEM] + [VMEM] * (2 + len(others)),
        out_specs=VMEM,
        scratch_shapes=[pltpu.VMEM((count, width), jnp.bfloat16)],
        input_output_aliases={3: 0},
        compiler_params=PARAMS,
        cost_estimate=cost(micros),
    )(scale, offset, low, total, *others)


def last_call(scale, offset, unit, recip, low, total, others, micros):
    rows, width = unit.shape
    count = sum(other.shape[0] for other in others)
    blocks = 4 if rows % 64 == 0 else 1
    return pl.pallas_call(
        functools.partial(last_kernel, len(others), blocks),
        out_shape=jax.ShapeDtypeStruct((rows, width), jnp.float32),
        in_specs=[SMEM, SMEM] + [VMEM] * (4 + len(others)),
        out_specs=pl.BlockSpec(memory_space=pl.ANY),
        scratch_shapes=[
            pltpu.VMEM((count, width), jnp.bfloat16),
            pltpu.VMEM((rows, width), jnp.float32),
            pltpu.SemaphoreType.DMA((blocks,)),
        ],
        compiler_params=PARAMS,
        cost_estimate=cost(micros),
    )(scale, offset, unit, recip, low, total, *others)


def unit_call(value):
    rows, width = value.shape
    return pl.pallas_call(
        unit_kernel,
        out_shape=(
            jax.ShapeDtypeStruct((rows, width), jnp.float32),
            jax.ShapeDtypeStruct((rows, 1), jnp.float32),
        ),
        in_specs=[VMEM],
        out_specs=(VMEM, VMEM),
        compiler_params=PARAMS,
        cost_estimate=cost(0.05),
    )(value)


def exchange(value, target):
    count = lax.axis_size(AXES)
    return lax.ppermute(value, AXES, [(at, target(at) % count) for at in range(count)])


def partner(at):
    return at ^ 1


def onward(at):
    return at + 2 if at % 2 == 0 else at - 2


def backward(at):
    return at - 2 if at % 2 == 0 else at + 2


def tied(value, *others):
    return lax.optimization_barrier((value, *others))[0]


def shards(images, texts, logit_scale, logit_bias):
    rows = images.shape[0]
    args = (logit_scale, logit_bias)

    def cut(value, start, stop):
        return value[rows * start // 32 : rows * stop // 32]

    tail = cut(images, 22, 32)
    lead = take_call(texts, rows * 11 // 32)
    near0 = exchange(lead, partner)
    near1 = exchange(tied(cut(texts, 11, 21), lead), partner)
    near2 = exchange(tied(cut(texts, 21, 32), lead), partner)
    near3 = exchange(tied(cut(images, 0, 11), lead), partner)
    side = exchange(tail, backward)
    img_low, txt_low, sum_img, sum_txt = own_call(*args, images, texts)
    far0 = exchange(near0, onward)
    near4 = exchange(tied(cut(images, 11, 22), near0), partner)
    far1 = exchange(tied(near1, img_low), onward)
    near_tail = exchange(tied(tail, near1), partner)
    far_tail = exchange(tied(side, near1), partner)
    sum_img = add_call(*args, img_low, tied(sum_img, side), (near1, near0,), 0.4)
    far2 = exchange(tied(near2, sum_img, far0), onward)
    sum_img = add_call(*args, img_low, sum_img, (near2,), 0.4)
    unit_img, recip_img = unit_call(tied(images, sum_img))
    unit_txt, recip_txt = unit_call(tied(texts, unit_img))
    far3 = exchange(tied(near3, unit_txt, unit_img, sum_img, far1), onward)
    sum_txt = add_call(*args, txt_low, sum_txt, (near3,), 0.4)
    far4 = exchange(tied(near4, sum_txt), onward)
    grad_img = last_call(*args, unit_img, recip_img, img_low, sum_img, (far0, far1, far2,), 0.05)
    sum_txt = add_call(*args, txt_low, tied(sum_txt, grad_img), (near4, far3,), 0.4)
    sum_txt = add_call(*args, txt_low, sum_txt, (near_tail,), 1.0)
    grad_txt = last_call(*args, unit_txt, recip_txt, txt_low, sum_txt, (far4, far_tail), 0.05)
    return grad_img, grad_txt


def solution(mesh):
    split = P(AXES, None)
    return jax.shard_map(
        shards,
        mesh=mesh,
        in_specs=(split, split, P(), P()),
        out_specs=(split, split),
        check_vma=False,
    )
```

```python
import functools

import jax
import jax.numpy as jnp
from jax import lax
from jax.experimental import pallas as pl
from jax.experimental.pallas import tpu as pltpu
from jax.sharding import PartitionSpec as P

AXES = ("blk", "sub")
LAST = (((1,), (1,)), ((), ()))
FIRST = (((0,), (0,)), ((), ()))
VMEM_LIMIT = 24 * 1024 * 1024


def unit_rows(values_in):
    values = values_in.astype(jnp.float32)
    recip = lax.rsqrt(jnp.sum(values * values, axis=-1, keepdims=True) + 1e-06)
    return values * recip, recip


def dot32(left, right, dims):
    return lax.dot_general(left, right, dims, preferred_element_type=jnp.float32)


def band_term(own_low, other_low, scale, offset):
    weight = jax.nn.sigmoid(scale * dot32(own_low, other_low, LAST) + offset)
    return jnp.dot(
        weight.astype(jnp.bfloat16), other_low, preferred_element_type=jnp.float32
    )


def take_kernel(value_ref, out_ref, sem):
    copy = pltpu.make_async_copy(value_ref.at[pl.ds(0, out_ref.shape[0]), :], out_ref, sem)
    copy.start()
    copy.wait()


def own_kernel(scale_ref, offset_ref, img_ref, txt_ref, img_low, txt_low, sum_img, sum_txt):
    scale, offset = scale_ref[0], offset_ref[0]
    lower_rows((img_ref,), img_low)
    lower_rows((txt_ref,), txt_low)
    logits = scale * dot32(img_low[...], txt_low[...], LAST) + offset
    rows = lax.broadcasted_iota(jnp.int32, logits.shape, 0)
    columns = lax.broadcasted_iota(jnp.int32, logits.shape, 1)
    weight = jax.nn.sigmoid(logits) - (rows == columns).astype(jnp.float32)
    weight = weight.astype(jnp.bfloat16)
    sum_img[...] = jnp.dot(weight, txt_low[...], preferred_element_type=jnp.float32)
    sum_txt[...] = dot32(weight, img_low[...], FIRST)


def lower_rows(others, other_low):
    at = 0
    for other in others:
        rows = other.shape[0]
        other_low[at : at + rows, :] = unit_rows(other[...])[0].astype(jnp.bfloat16)
        at += rows


def add_kernel(count, scale_ref, offset_ref, low_ref, sum_in, *rest):
    others, (sum_out, other_low) = rest[:count], rest[count:]
    scale, offset = scale_ref[0], offset_ref[0]
    lower_rows(others, other_low)
    sum_out[...] = sum_in[...] + band_term(low_ref[...], other_low[...], scale, offset)


def unit_kernel(value_ref, unit_ref, recip_ref):
    unit_ref[...], recip_ref[...] = unit_rows(value_ref[...])


def last_kernel(count, blocks, scale_ref, offset_ref, unit_ref, recip_ref, low_ref, sum_ref, *rest):
    others, (out_ref, other_low, held, sems) = rest[:count], rest[count:]
    scale, offset = scale_ref[0], offset_ref[0]
    lower_rows(others, other_low)
    half = (0.5 * scale) * dot32(low_ref[...], other_low[...], LAST) + 0.5 * offset
    weight = (0.5 * jnp.tanh(half) + 0.5).astype(jnp.bfloat16)
    size = held.shape[0] // blocks
    copies = []
    for block in range(blocks):
        start = block * size
        at = pl.ds(start, size)
        unit = unit_ref[at, :]
        term = jnp.dot(
            weight[start : start + size], other_low[...], preferred_element_type=jnp.float32
        )
        grad = scale * (sum_ref[at, :] + term)
        along = jnp.sum(unit * grad, axis=-1, keepdims=True)
        held[at, :] = (grad - unit * along) * recip_ref[at, :]
        copy = pltpu.make_async_copy(held.at[at, :], out_ref.at[at, :], sems.at[block])
        copy.start()
        copies.append(copy)
    for copy in copies:
        copy.wait()


def cost(micros):
    return pl.CostEstimate(flops=int(micros * 1e9), bytes_accessed=1024, transcendentals=0)


SMEM = pl.BlockSpec(memory_space=pltpu.SMEM)
VMEM = pl.BlockSpec(memory_space=pltpu.VMEM)
PARAMS = pltpu.CompilerParams(vmem_limit_bytes=VMEM_LIMIT)


def take_call(value, count):
    return pl.pallas_call(
        take_kernel,
        out_shape=jax.ShapeDtypeStruct((count, value.shape[1]), value.dtype),
        in_specs=[pl.BlockSpec(memory_space=pl.ANY)],
        out_specs=VMEM,
        scratch_shapes=[pltpu.SemaphoreType.DMA],
        compiler_params=PARAMS,
        cost_estimate=cost(0.8),
    )(value)


def own_call(scale, offset, images, texts):
    rows, width = texts.shape
    low = jax.ShapeDtypeStruct((rows, width), jnp.bfloat16)
    total = jax.ShapeDtypeStruct((rows, width), jnp.float32)
    return pl.pallas_call(
        own_kernel,
        out_shape=(low, low, total, total),
        in_specs=[SMEM, SMEM, VMEM, VMEM],
        out_specs=(VMEM,) * 4,
        compiler_params=PARAMS,
        cost_estimate=cost(0.8),
    )(scale, offset, images, texts)


def add_call(scale, offset, low, total, others, micros):
    rows, width = low.shape
    count = sum(other.shape[0] for other in others)
    return pl.pallas_call(
        functools.partial(add_kernel, len(others)),
        out_shape=jax.ShapeDtypeStruct((rows, width), jnp.float32),
        in_specs=[SMEM, SMEM] + [VMEM] * (2 + len(others)),
        out_specs=VMEM,
        scratch_shapes=[pltpu.VMEM((count, width), jnp.bfloat16)],
        input_output_aliases={3: 0},
        compiler_params=PARAMS,
        cost_estimate=cost(micros),
    )(scale, offset, low, total, *others)


def last_call(scale, offset, unit, recip, low, total, others, micros):
    rows, width = unit.shape
    count = sum(other.shape[0] for other in others)
    blocks = 4 if rows % 64 == 0 else 1
    return pl.pallas_call(
        functools.partial(last_kernel, len(others), blocks),
        out_shape=jax.ShapeDtypeStruct((rows, width), jnp.float32),
        in_specs=[SMEM, SMEM] + [VMEM] * (4 + len(others)),
        out_specs=pl.BlockSpec(memory_space=pl.ANY),
        scratch_shapes=[
            pltpu.VMEM((count, width), jnp.bfloat16),
            pltpu.VMEM((rows, width), jnp.float32),
            pltpu.SemaphoreType.DMA((blocks,)),
        ],
        compiler_params=PARAMS,
        cost_estimate=cost(micros),
    )(scale, offset, unit, recip, low, total, *others)


def unit_call(value):
    rows, width = value.shape
    return pl.pallas_call(
        unit_kernel,
        out_shape=(
            jax.ShapeDtypeStruct((rows, width), jnp.float32),
            jax.ShapeDtypeStruct((rows, 1), jnp.float32),
        ),
        in_specs=[VMEM],
        out_specs=(VMEM, VMEM),
        compiler_params=PARAMS,
        cost_estimate=cost(0.05),
    )(value)


def exchange(value, target):
    count = lax.axis_size(AXES)
    return lax.ppermute(value, AXES, [(at, target(at) % count) for at in range(count)])


def partner(at):
    return at ^ 1


def onward(at):
    return at + 2 if at % 2 == 0 else at - 2


def backward(at):
    return at - 2 if at % 2 == 0 else at + 2


def tied(value, *others):
    return lax.optimization_barrier((value, *others))[0]


def shards(images, texts, logit_scale, logit_bias):
    rows = images.shape[0]
    args = (logit_scale, logit_bias)

    def cut(value, start, stop):
        return value[rows * start // 32 : rows * stop // 32]

    tail = cut(images, 22, 32)
    lead = take_call(texts, rows * 11 // 32)
    near0 = exchange(lead, partner)
    near1 = exchange(tied(cut(texts, 11, 21), lead), partner)
    near2 = exchange(tied(cut(texts, 21, 32), lead), partner)
    near3 = exchange(tied(cut(images, 0, 11), lead), partner)
    side = exchange(tail, backward)
    img_low, txt_low, sum_img, sum_txt = own_call(*args, images, texts)
    far0 = exchange(near0, onward)
    near4 = exchange(tied(cut(images, 11, 22), near0), partner)
    far1 = exchange(tied(near1, img_low), onward)
    near_tail = exchange(tied(tail, near1), partner)
    far_tail = exchange(tied(side, near1), partner)
    sum_img = add_call(*args, img_low, tied(sum_img, side), (near1, near0,), 0.4)
    far2 = exchange(tied(near2, sum_img, far0), onward)
    sum_img = add_call(*args, img_low, sum_img, (near2,), 0.4)
    unit_img, recip_img = unit_call(tied(images, sum_img))
    unit_txt, recip_txt = unit_call(tied(texts, unit_img))
    far3 = exchange(tied(near3, unit_txt, unit_img, sum_img, far1), onward)
    sum_txt = add_call(*args, txt_low, sum_txt, (near3,), 0.4)
    far4 = exchange(tied(near4, sum_txt), onward)
    grad_img = last_call(*args, unit_img, recip_img, img_low, sum_img, (far0, far1, far2,), 0.05)
    sum_txt = add_call(*args, txt_low, tied(sum_txt, grad_img), (near4, far3,), 0.4)
    sum_txt = add_call(*args, txt_low, sum_txt, (near_tail,), 1.0)
    grad_txt = last_call(*args, unit_txt, recip_txt, txt_low, sum_txt, (far4, far_tail), 0.05)
    return grad_img, grad_txt


def solution(mesh):
    split = P(AXES, None)
    return jax.shard_map(
        shards,
        mesh=mesh,
        in_specs=(split, split, P(), P()),
        out_specs=(split, split),
        check_vma=False,
    )
```

```python
import functools

import jax
import jax.numpy as jnp
from jax import lax
from jax.experimental import pallas as pl
from jax.experimental.pallas import tpu as pltpu
from jax.sharding import PartitionSpec as P

AXES = ("blk", "sub")
LAST = (((1,), (1,)), ((), ()))
FIRST = (((0,), (0,)), ((), ()))
VMEM_LIMIT = 24 * 1024 * 1024


def unit_rows(values_in):
    values = values_in.astype(jnp.float32)
    recip = lax.rsqrt(jnp.sum(values * values, axis=-1, keepdims=True) + 1e-06)
    return values * recip, recip


def dot32(left, right, dims):
    return lax.dot_general(left, right, dims, preferred_element_type=jnp.float32)


def band_term(own_low, other_low, scale, offset):
    weight = jax.nn.sigmoid(scale * dot32(own_low, other_low, LAST) + offset)
    return jnp.dot(
        weight.astype(jnp.bfloat16), other_low, preferred_element_type=jnp.float32
    )


def take_kernel(value_ref, out_ref, sem):
    copy = pltpu.make_async_copy(value_ref.at[pl.ds(0, out_ref.shape[0]), :], out_ref, sem)
    copy.start()
    copy.wait()


def own_kernel(scale_ref, offset_ref, img_ref, txt_ref, img_low, txt_low, sum_img, sum_txt):
    scale, offset = scale_ref[0], offset_ref[0]
    lower_rows((img_ref,), img_low)
    lower_rows((txt_ref,), txt_low)
    logits = scale * dot32(img_low[...], txt_low[...], LAST) + offset
    rows = lax.broadcasted_iota(jnp.int32, logits.shape, 0)
    columns = lax.broadcasted_iota(jnp.int32, logits.shape, 1)
    weight = jax.nn.sigmoid(logits) - (rows == columns).astype(jnp.float32)
    weight = weight.astype(jnp.bfloat16)
    sum_img[...] = jnp.dot(weight, txt_low[...], preferred_element_type=jnp.float32)
    sum_txt[...] = dot32(weight, img_low[...], FIRST)


def lower_rows(others, other_low):
    at = 0
    for other in others:
        rows = other.shape[0]
        other_low[at : at + rows, :] = unit_rows(other[...])[0].astype(jnp.bfloat16)
        at += rows


def add_kernel(count, scale_ref, offset_ref, low_ref, sum_in, *rest):
    others, (sum_out, other_low) = rest[:count], rest[count:]
    scale, offset = scale_ref[0], offset_ref[0]
    lower_rows(others, other_low)
    sum_out[...] = sum_in[...] + band_term(low_ref[...], other_low[...], scale, offset)


def last_kernel(count, blocks, scale_ref, offset_ref, raw_ref, low_ref, sum_ref, *rest):
    others, (out_ref, other_low, held, sems) = rest[:count], rest[count:]
    scale, offset = scale_ref[0], offset_ref[0]
    lower_rows(others, other_low)
    logits = scale * dot32(low_ref[...], other_low[...], LAST) + offset
    weight = jax.nn.sigmoid(logits).astype(jnp.bfloat16)
    size = held.shape[0] // blocks
    copies = []
    for block in range(blocks):
        start = block * size
        at = pl.ds(start, size)
        unit, recip = unit_rows(raw_ref[at, :])
        term = jnp.dot(
            weight[start : start + size], other_low[...], preferred_element_type=jnp.float32
        )
        grad = scale * (sum_ref[at, :] + term)
        along = jnp.sum(unit * grad, axis=-1, keepdims=True)
        held[at, :] = (grad - unit * along) * recip
        copy = pltpu.make_async_copy(held.at[at, :], out_ref.at[at, :], sems.at[block])
        copy.start()
        copies.append(copy)
    for copy in copies:
        copy.wait()


def cost(micros):
    return pl.CostEstimate(flops=int(micros * 1e9), bytes_accessed=1024, transcendentals=0)


SMEM = pl.BlockSpec(memory_space=pltpu.SMEM)
VMEM = pl.BlockSpec(memory_space=pltpu.VMEM)
PARAMS = pltpu.CompilerParams(vmem_limit_bytes=VMEM_LIMIT)


def take_call(value, count):
    return pl.pallas_call(
        take_kernel,
        out_shape=jax.ShapeDtypeStruct((count, value.shape[1]), value.dtype),
        in_specs=[pl.BlockSpec(memory_space=pl.ANY)],
        out_specs=VMEM,
        scratch_shapes=[pltpu.SemaphoreType.DMA],
        compiler_params=PARAMS,
        cost_estimate=cost(0.8),
    )(value)


def own_call(scale, offset, images, texts):
    rows, width = texts.shape
    low = jax.ShapeDtypeStruct((rows, width), jnp.bfloat16)
    total = jax.ShapeDtypeStruct((rows, width), jnp.float32)
    return pl.pallas_call(
        own_kernel,
        out_shape=(low, low, total, total),
        in_specs=[SMEM, SMEM, VMEM, VMEM],
        out_specs=(VMEM,) * 4,
        compiler_params=PARAMS,
        cost_estimate=cost(0.8),
    )(scale, offset, images, texts)


def add_call(scale, offset, low, total, others, micros):
    rows, width = low.shape
    count = sum(other.shape[0] for other in others)
    return pl.pallas_call(
        functools.partial(add_kernel, len(others)),
        out_shape=jax.ShapeDtypeStruct((rows, width), jnp.float32),
        in_specs=[SMEM, SMEM] + [VMEM] * (2 + len(others)),
        out_specs=VMEM,
        scratch_shapes=[pltpu.VMEM((count, width), jnp.bfloat16)],
        input_output_aliases={3: 0},
        compiler_params=PARAMS,
        cost_estimate=cost(micros),
    )(scale, offset, low, total, *others)


def last_call(scale, offset, raw, low, total, others, micros):
    rows, width = raw.shape
    count = sum(other.shape[0] for other in others)
    blocks = 4 if rows % 64 == 0 else 1
    return pl.pallas_call(
        functools.partial(last_kernel, len(others), blocks),
        out_shape=jax.ShapeDtypeStruct((rows, width), jnp.float32),
        in_specs=[SMEM, SMEM] + [VMEM] * (3 + len(others)),
        out_specs=pl.BlockSpec(memory_space=pl.ANY),
        scratch_shapes=[
            pltpu.VMEM((count, width), jnp.bfloat16),
            pltpu.VMEM((rows, width), jnp.float32),
            pltpu.SemaphoreType.DMA((blocks,)),
        ],
        compiler_params=PARAMS,
        cost_estimate=cost(micros),
    )(scale, offset, raw, low, total, *others)


def exchange(value, target):
    count = lax.axis_size(AXES)
    return lax.ppermute(value, AXES, [(at, target(at) % count) for at in range(count)])


def partner(at):
    return at ^ 1


def onward(at):
    return at + 2 if at % 2 == 0 else at - 2


def backward(at):
    return at - 2 if at % 2 == 0 else at + 2


def tied(value, *others):
    return lax.optimization_barrier((value, *others))[0]


def shards(images, texts, logit_scale, logit_bias):
    rows = images.shape[0]
    args = (logit_scale, logit_bias)

    def cut(value, start, stop):
        return value[rows * start // 32 : rows * stop // 32]

    tail = cut(images, 22, 32)
    lead = take_call(texts, rows * 11 // 32)
    near0 = exchange(lead, partner)
    near1 = exchange(tied(cut(texts, 11, 21), lead), partner)
    near2 = exchange(tied(cut(texts, 21, 32), lead), partner)
    near3 = exchange(tied(cut(images, 0, 11), lead), partner)
    side = exchange(tail, backward)
    img_low, txt_low, sum_img, sum_txt = own_call(*args, images, texts)
    far0 = exchange(near0, onward)
    near4 = exchange(tied(cut(images, 11, 22), near0), partner)
    far1 = exchange(tied(near1, img_low), onward)
    near_tail = exchange(tied(tail, near1), partner)
    far_tail = exchange(tied(side, near1), partner)
    sum_img = add_call(*args, img_low, tied(sum_img, side), (near1, near0,), 0.4)
    far2 = exchange(tied(near2, sum_img, far0), onward)
    sum_img = add_call(*args, img_low, sum_img, (near2,), 0.4)
    far3 = exchange(tied(near3, sum_img, far1), onward)
    sum_txt = add_call(*args, txt_low, sum_txt, (near3,), 0.4)
    far4 = exchange(tied(near4, sum_txt), onward)
    grad_img = last_call(*args, images, img_low, sum_img, (far0, far1, far2,), 0.05)
    sum_txt = add_call(*args, txt_low, tied(sum_txt, grad_img), (near4, far3, near_tail), 0.4)
    grad_txt = last_call(*args, texts, txt_low, sum_txt, (far4, far_tail), 0.05)
    return grad_img, grad_txt


def solution(mesh):
    split = P(AXES, None)
    return jax.shard_map(
        shards,
        mesh=mesh,
        in_specs=(split, split, P(), P()),
        out_specs=(split, split),
        check_vma=False,
    )
```
